128 devices in a mesh: row: 16 (over y, z_hi, core), col: 8 (over x, z_lo).
Axes of the slice: x: 4, y: 4, z: 4 (z_hi: 2, z_lo: 2; z = z_hi * 2 + z_lo), core: 2. Of those that a mesh axis runs over, the one named last changes fastest.
Arguments:
- activations: bfloat16 [4096, 4096], P(('row', 'col')), may hold values from -6 to 6
- grad_gate: bfloat16 [4096, 14336], P(('row', 'col')), may hold values from -6 to 6
- grad_up: bfloat16 [4096, 14336], P(('row', 'col')), may hold values from -6 to 6
- doc_order: int32 [16], replicated, may hold values from 0 to 15, each once
- seeds: int32 [2], replicated, may hold values from 0 to 1073741823
Outputs:
- sketches: float32 [2, 16, 128], P(None, 'row', 'col')
The draws below stay inside these ranges and needn't reach their ends.
Inputs may be any that keep to these rules, and one draw needn't show every extreme that they name: `doc_order`: each document appears once.
All inputs are finite; a program needn't handle non-finite values.
Results may differ from the reference program's by a relative error of at most 0.0029.
Values may be sent and summed in bfloat16 or wider, within the bound.
A program may use at most 128 MiB of HBM per device.

```python
import math
import jax
import jax.numpy as jnp
from jax import lax

D = 4096
FF = 14336
K = 128
SEQ = 256
DOCS = 16
TOKENS = 4096


def shard_levels(key, extent, pieces, smallest, largest):
    def one(position, blocks):
        steps = jax.random.uniform(jax.random.fold_in(jax.random.fold_in(key, 6), position), (blocks,), jnp.float32, smallest / len(pieces), largest / len(pieces))
        return jnp.repeat(jnp.exp(steps), extent[position] // blocks).reshape((-1,) + (1,) * (len(extent) - position - 1))

    level = one(*pieces[0])
    for cut in pieces[1:]:
        level = level * one(*cut)
    return level


def noise(own_key, dims, spread, most, split=(), kind=jnp.bfloat16):
    values = jax.random.normal(own_key, dims, jnp.float32) * spread
    if len(split) > 0:
        values = shard_levels(own_key, dims, split, -0.22, 0.18) * values
    return jnp.clip(values, min=-most, max=most).astype(kind)


def setup_inputs(seed: int = 0) -> dict:
    arg_keys = jax.random.split(jax.random.key(seed), 6)
    activations = noise(arg_keys[0], (TOKENS, D), 1.0, 6.0, ((0, 128),))
    grad_gate = noise(arg_keys[1], (TOKENS, FF), 1.0, 6.0, ((0, 128),))
    grad_up = noise(arg_keys[2], (TOKENS, FF), 1.0, 6.0, ((0, 128),))
    doc_order = jax.random.permutation(arg_keys[3], DOCS).astype(jnp.int32)
    seeds = jax.random.randint(arg_keys[4], (2,), 0, 1073741824).astype(jnp.int32)
    return dict(activations=activations, grad_gate=grad_gate, grad_up=grad_up, doc_order=doc_order, seeds=seeds)


def hash_mix(value_in):
    value_in = value_in ^ lax.shift_right_logical(value_in, jnp.full_like(value_in, 16))
    value_in = value_in * -2048144789
    value_in = value_in ^ lax.shift_right_logical(value_in, jnp.full_like(value_in, 13))
    value_in = value_in * -1028477387
    value_in = value_in ^ lax.shift_right_logical(value_in, jnp.full_like(value_in, 16))
    return value_in

def hashed_signs(row_begin, row_count, col_begin, col_count, row_width, seed_value):
    row_ids = row_begin + jnp.arange(row_count, dtype=jnp.int32)
    col_ids = col_begin + jnp.arange(col_count, dtype=jnp.int32)
    counter = row_ids[:, None] * row_width + col_ids[None, :]
    word_count = K // 32
    hashed = hash_mix(hash_mix(counter[:, :, None] * word_count + jnp.arange(word_count, dtype=jnp.int32)) + seed_value)
    full_shape = (row_count, col_count, word_count, 32)
    shifted = lax.shift_right_logical(jnp.broadcast_to(hashed[:, :, :, None], full_shape), jnp.broadcast_to(jnp.arange(32, dtype=jnp.int32), full_shape))
    sign_bits = (shifted & 1).reshape(row_count, col_count, K)
    return jnp.where(sign_bits == 1, -1.0, 1.0).astype(jnp.bfloat16)

def reference(activations, grad_gate, grad_up, doc_order, seeds):
    doc_count = activations.shape[0] // SEQ
    tokens_f = activations.astype(jnp.float32).reshape(doc_count, SEQ, D)
    row_block = math.gcd(FF, 64)
    scale = 1.0 / math.sqrt(SEQ * D * FF)
    onehot = (doc_order[None, :] == jnp.arange(doc_count, dtype=jnp.int32)[:, None]).astype(jnp.float32)
    results = []
    for matrix_id, grads in enumerate((grad_gate, grad_up)):
        grads_f = grads.astype(jnp.float32).reshape(doc_count, SEQ, FF)
        seed_value = seeds[matrix_id]

        def one_block(begin_row):
            picked = lax.dynamic_slice_in_dim(grads_f, begin_row, row_block, 2)
            gradient = jnp.einsum('ntr,ntc->nrc', picked, tokens_f, precision=lax.Precision.HIGHEST).astype(jnp.bfloat16)
            signs_here = hashed_signs(begin_row, row_block, 0, D, D, seed_value)
            return jnp.einsum('nrc,rck->nk', gradient.astype(jnp.float32), signs_here.astype(jnp.float32), precision=lax.Precision.HIGHEST)
        starts = jnp.arange(0, FF, row_block, dtype=jnp.int32)
        partial_sums = lax.optimization_barrier(jnp.sum(lax.map(one_block, starts), axis=0))
        placed = jnp.dot(onehot, partial_sums, precision=lax.Precision.HIGHEST)
        results.append(placed * scale)
    return jnp.stack(results)
```

```python
import functools
import math

import jax
import jax.numpy as jnp
from jax import lax
from jax.experimental import pallas as pl
from jax.experimental.pallas import tpu as pltpu
from jax.sharding import PartitionSpec as P

D = 4096
FF = 14336
K = 128
SEQ = 256
MESH = pl.DeviceIdType.MESH
BF16 = jnp.bfloat16
ROWS = 896
COLS = 1024
CH = 128
NQ = ROWS // CH
NP = 2
PW = COLS // NP


def lsr(value, count):
    return lax.shift_right_logical(value, jnp.full_like(value, count))


def hash_mix(v):
    v = v ^ lsr(v, 16)
    v = v * -2048144789
    v = v ^ lsr(v, 13)
    v = v * -1028477387
    return v ^ lsr(v, 16)


def device_of(x, y, z, k):
    return (y * 4 + (z // 2) * 2 + k, x * 2 + lax.rem(z, 2))


def kernel(
    act_in, gate_in, up_in, order_ref, seed_ref, out_ref,
    acts, grads, words, gs, acc, part, fin1, mid, fin2,
    r_s0, r_s1, r_s2, r_s3, r_a2a, r_ring, r_f1, r_f2,
    s_s0, s_s1, s_s2, s_s3, s_a2a, s_ring, s_f1, s_f2,
):
    row = lax.axis_index("row")
    col = lax.axis_index("col")
    y = row // 4
    zh = lax.rem(row // 2, 2)
    k = lax.rem(row, 2)
    x = col // 2
    zl = lax.rem(col, 2)
    z = zh * 2 + zl
    me = (y * 4 + z) * 2 + k

    def at_x(dx):
        return device_of(lax.rem(x + dx, 4), y, z, k)

    def at_y(dy):
        return device_of(x, lax.rem(y + dy, 4), z, k)

    def at_z(dz):
        return device_of(x, y, lax.rem(z + dz, 4), k)

    sibling = device_of(x, y, z, 1 - k)

    barrier = pltpu.get_barrier_semaphore()

    def greet(j, _):
        t = lax.rem(me + j, 32)
        pl.semaphore_signal(
            barrier, inc=1, device_id=device_of(x, t // 8, lax.rem(t // 2, 4), lax.rem(t, 2)), device_id_type=MESH
        )
        return 0

    lax.fori_loop(1, 32, greet, 0)
    for dx in range(1, 4):
        for dz in range(2):
            pl.semaphore_signal(
                barrier, inc=1,
                device_id=(row, lax.rem(x + dx, 4) * 2 + lax.rem(zl + dz, 2)), device_id_type=MESH,
            )
    pl.semaphore_wait(barrier, 37)

    def remote(src, dst, send, recv, target):
        return pltpu.make_async_remote_copy(
            src_ref=src, dst_ref=dst, send_sem=send, recv_sem=recv, device_id=target, device_id_type=MESH
        )

    def arrive(ref, sem):
        pltpu.make_async_copy(ref, ref, sem).wait()

    def act_slice(c):
        return lambda p: act_in.at[:, pl.ds(pl.multiple_of(c * COLS + p * PW, PW), PW)]

    def s0(p):
        own = acts.at[p, k, zh, y, x, zl]
        pltpu.make_async_copy(act_slice(x)(p), own, r_s0.at[p]).start()
        for dx in range(1, 4):
            c = lax.rem(x + dx, 4)
            remote(act_slice(c)(p), own, s_s0.at[p, dx - 1], r_s0.at[p], at_x(dx)).start()

    def s0_done(p):
        for dx in range(1, 4):
            own = acts.at[p, k, zh, y, x, zl]
            remote(act_slice(lax.rem(x + dx, 4))(p), own, s_s0.at[p, dx - 1], r_s0.at[p], at_x(dx)).wait_send()

    def s1_copy(p, i, target):
        block = acts.at[p, k, zh, y, :, zl]
        return remote(block, block, s_s1.at[p, i - 1], r_s1.at[p], target)

    def s1(p):
        arrive(acts.at[p, 0, 0, 0, :, 0], r_s0.at[p])

        @pl.when(k == 0)
        def _():
            for i in range(1, 4):
                s1_copy(p, i, at_y(i)).start()

        @pl.when(k == 1)
        def _():
            for i in range(1, 4):
                s1_copy(p, i, at_z(i)).start()

    def line(p, core, step, half=None):
        if core == 0:
            zz = lax.rem(z + step, 4)
            ys = pl.ds(0, 4) if half is None else pl.ds(half * 2, 2)
            return acts.at[p, 0, zz // 2, ys, :, lax.rem(zz, 2)]
        yy = lax.rem(y + step, 4)
        if half is None:
            return acts.at[p, 1, :, yy]
        return acts.at[p, 1, half, yy]

    def nxt(core, step):
        return at_z(step) if core == 0 else at_y(step)

    def s2_copy(p, core, which):
        ref = [line(p, core, 0), line(p, core, 0), line(p, core, 3, 0), line(p, core, 1, 1)][which]
        return remote(ref, ref, s_s2.at[p, which], r_s2.at[p, which], nxt(core, 1 if which % 2 == 0 else 3))

    def s3_copy(p, core, which):
        ref = [
            line(p, core, 0), line(p, core, 3), line(p, core, 1), line(p, core, 2, 0), line(p, core, 2, 1)
        ][which]
        return remote(ref, ref, s_s3.at[p, which], r_s3.at[p], sibling)

    def by_core(f):
        @pl.when(k == 0)
        def _():
            f(0)

        @pl.when(k == 1)
        def _():
            f(1)

    full = lambda p: acts.at[p, 0, 0, :, :, 0]
    half = lambda p: acts.at[p, 0, 0, pl.ds(0, 2), :, 0]

    def s2(p):
        arrive(acts.at[p, 0, 0, pl.ds(0, 3), :, 0], r_s1.at[p])

        def go(core):
            s2_copy(p, core, 0).start()
            s2_copy(p, core, 1).start()
            s3_copy(p, core, 0).start()

        by_core(go)

    def s2_on(p):
        arrive(full(p), r_s2.at[p, 0])

        def go_left(core):
            s2_copy(p, core, 2).start()
            s3_copy(p, core, 1).start()

        by_core(go_left)
        arrive(full(p), r_s2.at[p, 1])

        def go_right(core):
            s2_copy(p, core, 3).start()
            s3_copy(p, core, 2).start()

        by_core(go_right)

    def s3(p):
        arrive(half(p), r_s2.at[p, 2])
        by_core(lambda core: s3_copy(p, core, 3).start())
        arrive(half(p), r_s2.at[p, 3])
        by_core(lambda core: s3_copy(p, core, 4).start())

    def act_ready(p):
        arrive(acts.at[p, 0], r_s3.at[p])

    def act_done(p):
        s0_done(p)

        def go(core):
            for i in range(1, 4):
                s1_copy(p, i, at_y(i) if core == 0 else at_z(i)).wait_send()
            for w in range(4):
                s2_copy(p, core, w).wait_send()
            for w in range(5):
                s3_copy(p, core, w).wait_send()

        by_core(go)

    def a2a(q):
        dst = grads.at[q, k, zh, y, x, zl]

        def send(j, _):
            t = lax.rem(me // 2 + j, 16)
            begin = pl.multiple_of(t * ROWS + q * CH, CH)
            ty = t // 4
            tz = lax.rem(t, 4)

            @pl.when((j > 0) | (k == 1))
            def _():
                remote(
                    gate_in.at[:, pl.ds(begin, CH)], dst, s_a2a.at[q], r_a2a.at[q], device_of(x, ty, tz, 0)
                ).start()

            @pl.when((j > 0) | (k == 0))
            def _():
                remote(
                    up_in.at[:, pl.ds(begin, CH)], dst, s_a2a.at[q], r_a2a.at[q], device_of(x, ty, tz, 1)
                ).start()

            return 0

        begin = pl.multiple_of((me // 2) * ROWS + q * CH, CH)

        @pl.when(k == 0)
        def _():
            pltpu.make_async_copy(gate_in.at[:, pl.ds(begin, CH)], dst, r_a2a.at[q]).start()

        @pl.when(k == 1)
        def _():
            pltpu.make_async_copy(up_in.at[:, pl.ds(begin, CH)], dst, r_a2a.at[q]).start()

        lax.fori_loop(0, 16, send, 0)

    def ring_copy(q, which):
        at = [0, 0, 3, 1][which]
        xx = lax.rem(x + at, 4)
        ref = grads.at[q, :, :, :, xx] if which < 2 else grads.at[q, which - 2, :, :, xx]
        return remote(ref, ref, s_ring.at[q, which], r_ring.at[q, which], at_x(1 if which % 2 == 0 else 3))

    def ring(q):
        arrive(grads.at[q, :, :, :, 0], r_a2a.at[q])
        ring_copy(q, 0).start()
        ring_copy(q, 1).start()

    def ring_on(q):
        arrive(grads.at[q, :, :, :, 0], r_ring.at[q, 0])
        ring_copy(q, 2).start()
        arrive(grads.at[q, :, :, :, 0], r_ring.at[q, 1])
        ring_copy(q, 3).start()

    def grad_ready(q):
        arrive(grads.at[q, 0, :, :, 0], r_ring.at[q, 2])
        arrive(grads.at[q, 0, :, :, 0], r_ring.at[q, 3])

    def grad_done(q, _):
        sent = gate_in.at[:, pl.ds(0, 31 * CH)]
        pltpu.make_async_copy(sent, sent, s_a2a.at[q]).wait()
        for w in range(4):
            ring_copy(q, w).wait_send()
        return 0

    seed = jnp.where(k == 0, seed_ref[0], seed_ref[1])
    row_base = (y * 4 + z) * ROWS
    col_base = x * COLS

    def hash_chunk(q):
        it = lax.broadcasted_iota(jnp.int32, (8, COLS), 0)
        jt = lax.broadcasted_iota(jnp.int32, (8, COLS), 1)
        base = ((row_base + lsr(it, 2)) * D + col_base + jt) * 4 + (it & 3)

        def two_rows(t, _):
            for u in range(2):
                tt = q * (CH // 2) + t * 2 + u
                h = hash_mix(hash_mix(base + tt * (2 * D * 4)) + seed)
                words[tt] = jnp.concatenate([h, lsr(h, 16)], 0).astype(jnp.int16)
            return 0

        lax.fori_loop(0, CH // 4, two_rows, 0)

    pair_of = lsr(lax.broadcasted_iota(jnp.int32, (256, 256), 1) & 15, 1)

    def work(q, p_lo, p_hi):
        def eight_docs(d, _):
            for c in range(2):
                for yy in range(4):
                    gt = grads[q, d, c, yy].reshape(SEQ, CH).T
                    for p in range(p_lo, p_hi):
                        a = acts[p, d, c, yy].reshape(SEQ, PW)
                        g = jnp.dot(gt, a, preferred_element_type=jnp.float32)
                        gs[d * 8 + c * 4 + yy, :, p * PW:(p + 1) * PW] = g.astype(BF16)
            return 0

        lax.fori_loop(0, 2, eight_docs, 0)
        lo, hi = p_lo * PW, p_hi * PW

        def rows_32(t, _):
            for v in range(2):
                begin = pl.multiple_of(t * 32 + v * 16, 16)
                g = jnp.concatenate([gs[n, pl.ds(begin, 16), lo:hi] for n in range(16)], 0)
                picked = None
                for pair in range(8):
                    w = words[q * (CH // 2) + t * 16 + v * 8 + pair, :, lo:hi]
                    s = jnp.concatenate(
                        [
                            jnp.where(
                                (w & jnp.int16((1 << b) if b < 15 else -32768)) != 0, BF16(-1.0), BF16(1.0)
                            )
                            for b in range(16)
                        ],
                        0,
                    )
                    r = lax.dot_general(s, g, (((1,), (1,)), ((), ())), preferred_element_type=jnp.float32)
                    picked = r if picked is None else jnp.where(pair_of == pair, r, picked)
                acc[...] += picked
            return 0

        lax.fori_loop(0, CH // 32, rows_32, 0)

    acc[...] = jnp.zeros_like(acc)
    s0(0)
    a2a(0)
    s0(1)
    s1(0)
    s1(1)
    a2a(1)
    hash_chunk(0)
    s2(0)
    ring(0)
    s2(1)
    hash_chunk(1)
    hash_chunk(2)
    s2_on(0)
    ring(1)
    hash_chunk(3)
    s3(0)
    ring_on(0)
    s2_on(1)
    a2a(2)
    hash_chunk(4)
    a2a(3)
    s3(1)
    act_ready(0)
    grad_ready(0)
    ring_on(1)
    work(0, 0, 1)
    a2a(4)
    ring(2)
    grad_ready(1)
    work(1, 0, 1)
    act_ready(1)
    a2a(5)
    a2a(6)
    work(0, 1, 2)
    ring_on(2)
    ring(3)
    work(1, 1, 2)
    hash_chunk(5)
    hash_chunk(6)

    def chunk(q, _):
        grad_ready(q)

        @pl.when(q + 1 < NQ)
        def _():
            ring_on(q + 1)

        @pl.when(q + 2 < NQ)
        def _():
            ring(q + 2)

        work(q, 0, 2)
        return 0

    lax.fori_loop(2, NQ, chunk, 0)

    ri = lax.broadcasted_iota(jnp.int32, (256, 256), 0)
    ci = lax.broadcasted_iota(jnp.int32, (256, 256), 1)
    kept = jnp.where((lsr(ri, 2) & 1) == (ci & 1), acc[...], 0.0)
    cf = lsr(lax.broadcasted_iota(jnp.int32, (256, 16), 0), 4)
    df = lax.broadcasted_iota(jnp.int32, (256, 16), 1)
    fold = jnp.zeros((256, 16), jnp.float32)
    for n in range(16):
        doc = order_ref[(n % 4) * 4 + ((n // 4) % 2) * 2 + n // 8]
        fold = jnp.where((cf == n) & (df == doc), 1.0, fold)
    rk = lax.broadcasted_iota(jnp.int32, (256, 128), 0)
    ck = lax.broadcasted_iota(jnp.int32, (256, 128), 1)
    place = jnp.where((rk & 3) * 32 + (lsr(rk, 3) & 1) * 16 + lsr(rk, 4) == ck, 1.0, 0.0)
    by_doc = jnp.dot(kept, fold, precision=lax.Precision.HIGHEST, preferred_element_type=jnp.float32)
    mine = lax.dot_general(
        by_doc, place, (((0,), (0,)), ((), ())),
        precision=lax.Precision.HIGHEST, preferred_element_type=jnp.float32,
    )
    for d in range(16):
        part[d] = jnp.broadcast_to(mine[d:d + 1, :], (8, 128))

    def f1_copy(j):
        t = lax.rem(row + j, 16)
        return remote(part.at[t], fin1.at[row], s_f1, r_f1, (t, col))

    pltpu.make_async_copy(part.at[row], fin1.at[row], r_f1).start()
    lax.fori_loop(1, 16, lambda j, _: (f1_copy(j).start(), 0)[1], 0)
    arrive(fin1, r_f1)
    for m in range(2):
        total = fin1[m]
        for r in range(1, 8):
            total = total + fin1[r * 2 + m]
        mid[m] = total

    def f2_copy(j):
        return remote(mid, fin2.at[col], s_f2.at[j - 1], r_f2, (row, lax.rem(col + j, 8)))

    pltpu.make_async_copy(mid, fin2.at[col], r_f2).start()
    for j in range(1, 8):
        f2_copy(j).start()
    arrive(fin2, r_f2)
    total = fin2[0]
    for c in range(1, 8):
        total = total + fin2[c]
    out_ref[...] = total * (1.0 / math.sqrt(SEQ * D * FF))

    for p in range(NP):
        act_done(p)
    lax.fori_loop(0, NQ, grad_done, 0)
    sent = part.at[pl.ds(0, 15)]
    pltpu.make_async_copy(sent, sent, s_f1).wait()
    for j in range(1, 8):
        f2_copy(j).wait_send()


def shards(activations, grad_gate, grad_up, doc_order, seeds):
    dma = pltpu.SemaphoreType.DMA
    total = pl.pallas_call(
        kernel,
        out_shape=jax.ShapeDtypeStruct((2, 8, K), jnp.float32),
        in_specs=[pl.BlockSpec(memory_space=pl.ANY)] * 3 + [pl.BlockSpec(memory_space=pltpu.SMEM)] * 2,
        out_specs=pl.BlockSpec(memory_space=pltpu.VMEM),
        scratch_shapes=[
            pltpu.VMEM((NP, 2, 2, 4, 4, 2, 32, PW), BF16),
            pltpu.VMEM((NQ, 2, 2, 4, 4, 2, 32, CH), BF16),
            pltpu.VMEM((ROWS // 2, 16, COLS), jnp.int16),
            pltpu.VMEM((16, CH, COLS), BF16),
            pltpu.VMEM((256, 256), jnp.float32),
            pltpu.VMEM((16, 8, K), jnp.float32),
            pltpu.VMEM((16, 8, K), jnp.float32),
            pltpu.VMEM((2, 8, K), jnp.float32),
            pltpu.VMEM((8, 2, 8, K), jnp.float32),
            dma((NP,)), dma((NP,)), dma((NP, 4)), dma((NP,)), dma((NQ,)), dma((NQ, 4)), dma, dma,
            dma((NP, 3)), dma((NP, 3)), dma((NP, 4)), dma((NP, 5)), dma((NQ,)), dma((NQ, 4)), dma, dma((7,)),
        ],
        compiler_params=pltpu.CompilerParams(
            collective_id=0, has_side_effects=True, vmem_limit_bytes=56 * 2**20
        ),
        name="sketch",
    )(activations, grad_gate, grad_up, doc_order, seeds)
    col = lax.axis_index("col")
    return lax.dynamic_slice(total, (jnp.int32(0), jnp.int32(0), col * 16), (2, 1, 16))


def solution(mesh):
    in_specs = (P(("row", "col"), None), P(("row", "col"), None), P(("row", "col"), None), P(), P())
    out_specs = P(None, "row", "col")
    return jax.shard_map(shards, mesh=mesh, in_specs=in_specs, out_specs=out_specs, check_vma=False)
```

```python
import functools
import math

import jax
import jax.numpy as jnp
from jax import lax
from jax.experimental import pallas as pl
from jax.experimental.pallas import tpu as pltpu
from jax.sharding import PartitionSpec as P

D = 4096
FF = 14336
K = 128
SEQ = 256
MESH = pl.DeviceIdType.MESH
BF16 = jnp.bfloat16
ROWS = 896
COLS = 1024
CH = 128
NQ = ROWS // CH
PIECE = (256, 256, 512)
BEGIN = (0, 256, 512)
NP = 3


def lsr(value, count):
    return lax.shift_right_logical(value, jnp.full_like(value, count))


def hash_mix(v):
    v = v ^ lsr(v, 16)
    v = v * -2048144789
    v = v ^ lsr(v, 13)
    v = v * -1028477387
    return v ^ lsr(v, 16)


def device_of(x, y, z, k):
    return (y * 4 + (z // 2) * 2 + k, x * 2 + lax.rem(z, 2))


def kernel(
    act_in, gate_in, up_in, order_ref, seed_ref, out_ref,
    acts0, acts1, acts2, grads, words, gs, acc, part, fin1, mid, fin2,
    r_s0, r_s1, r_s2, r_s3, r_a2a, r_ring, r_f1, r_f2,
    s_s0, s_s1, s_s2, s_s3, s_a2a, s_ring, s_f1, s_f2,
):
    acts = (acts0, acts1, acts2)
    row = lax.axis_index("row")
    col = lax.axis_index("col")
    y = row // 4
    zh = lax.rem(row // 2, 2)
    k = lax.rem(row, 2)
    x = col // 2
    zl = lax.rem(col, 2)
    z = zh * 2 + zl
    me = (y * 4 + z) * 2 + k

    def at_x(dx):
        return device_of(lax.rem(x + dx, 4), y, z, k)

    def at_y(dy):
        return device_of(x, lax.rem(y + dy, 4), z, k)

    def at_z(dz):
        return device_of(x, y, lax.rem(z + dz, 4), k)

    sibling = device_of(x, y, z, 1 - k)

    barrier = pltpu.get_barrier_semaphore()

    def greet(j, _):
        t = lax.rem(me + j, 32)
        pl.semaphore_signal(
            barrier, inc=1, device_id=device_of(x, t // 8, lax.rem(t // 2, 4), lax.rem(t, 2)), device_id_type=MESH
        )
        return 0

    lax.fori_loop(1, 32, greet, 0)
    for dx in range(1, 4):
        for dz in range(2):
            pl.semaphore_signal(
                barrier, inc=1,
                device_id=(row, lax.rem(x + dx, 4) * 2 + lax.rem(zl + dz, 2)), device_id_type=MESH,
            )
    seed = jnp.where(k == 0, seed_ref[0], seed_ref[1])
    row_base = (y * 4 + z) * ROWS
    col_base = x * COLS

    def hash_chunk(q):
        it = lax.broadcasted_iota(jnp.int32, (8, COLS), 0)
        jt = lax.broadcasted_iota(jnp.int32, (8, COLS), 1)
        base = ((row_base + lsr(it, 2)) * D + col_base + jt) * 4 + (it & 3)

        def two_rows(t, _):
            for u in range(2):
                tt = q * (CH // 2) + t * 2 + u
                h = hash_mix(hash_mix(base + tt * (2 * D * 4)) + seed)
                words[tt] = jnp.concatenate([h, lsr(h, 16)], 0).astype(jnp.int16)
            return 0

        lax.fori_loop(0, CH // 4, two_rows, 0)

    hash_chunk(0)
    hash_chunk(1)
    pl.semaphore_wait(barrier, 37)

    def remote(src, dst, send, recv, target):
        return pltpu.make_async_remote_copy(
            src_ref=src, dst_ref=dst, send_sem=send, recv_sem=recv, device_id=target, device_id_type=MESH
        )

    def arrive(ref, sem):
        pltpu.make_async_copy(ref, ref, sem).wait()

    def act_slice(c):
        return lambda p: act_in.at[:, pl.ds(pl.multiple_of(c * COLS + BEGIN[p], 256), PIECE[p])]

    def s0(p):
        own = acts[p].at[k, zh, y, x, zl]
        pltpu.make_async_copy(act_slice(x)(p), own, r_s0.at[p]).start()
        for dx in range(1, 4):
            c = lax.rem(x + dx, 4)
            remote(act_slice(c)(p), own, s_s0.at[p, dx - 1], r_s0.at[p], at_x(dx)).start()

    def s0_done(p):
        for dx in range(1, 4):
            own = acts[p].at[k, zh, y, x, zl]
            remote(act_slice(lax.rem(x + dx, 4))(p), own, s_s0.at[p, dx - 1], r_s0.at[p], at_x(dx)).wait_send()

    def s1_copy(p, i, target):
        block = acts[p].at[k, zh, y, :, zl]
        return remote(block, block, s_s1.at[p, i - 1], r_s1.at[p], target)

    def s1(p):
        arrive(acts[p].at[0, 0, 0, :, 0], r_s0.at[p])

        @pl.when(k == 0)
        def _():
            for i in range(1, 4):
                s1_copy(p, i, at_y(i)).start()

        @pl.when(k == 1)
        def _():
            for i in range(1, 4):
                s1_copy(p, i, at_z(i)).start()

    def line(p, core, step, half=None):
        if core == 0:
            zz = lax.rem(z + step, 4)
            ys = pl.ds(0, 4) if half is None else pl.ds(half * 2, 2)
            return acts[p].at[0, zz // 2, ys, :, lax.rem(zz, 2)]
        yy = lax.rem(y + step, 4)
        if half is None:
            return acts[p].at[1, :, yy]
        return acts[p].at[1, half, yy]

    def nxt(core, step):
        return at_z(step) if core == 0 else at_y(step)

    def s2_copy(p, core, which):
        ref = [line(p, core, 0), line(p, core, 0), line(p, core, 3, 0), line(p, core, 1, 1)][which]
        return remote(ref, ref, s_s2.at[p, which], r_s2.at[p, which], nxt(core, 1 if which % 2 == 0 else 3))

    def s3_copy(p, core, which):
        ref = [
            line(p, core, 0), line(p, core, 3), line(p, core, 1), line(p, core, 2, 0), line(p, core, 2, 1)
        ][which]
        return remote(ref, ref, s_s3.at[p, which], r_s3.at[p], sibling)

    def by_core(f):
        @pl.when(k == 0)
        def _():
            f(0)

        @pl.when(k == 1)
        def _():
            f(1)

    full = lambda p: acts[p].at[0, 0, :, :, 0]
    half = lambda p: acts[p].at[0, 0, pl.ds(0, 2), :, 0]

    def s2(p):
        arrive(acts[p].at[0, 0, pl.ds(0, 3), :, 0], r_s1.at[p])

        def go(core):
            s2_copy(p, core, 0).start()
            s2_copy(p, core, 1).start()
            s3_copy(p, core, 0).start()

        by_core(go)

    def s2_on(p):
        arrive(full(p), r_s2.at[p, 0])

        def go_left(core):
            s2_copy(p, core, 2).start()
            s3_copy(p, core, 1).start()

        by_core(go_left)
        arrive(full(p), r_s2.at[p, 1])

        def go_right(core):
            s2_copy(p, core, 3).start()
            s3_copy(p, core, 2).start()

        by_core(go_right)

    def s3(p):
        arrive(half(p), r_s2.at[p, 2])
        by_core(lambda core: s3_copy(p, core, 3).start())
        arrive(half(p), r_s2.at[p, 3])
        by_core(lambda core: s3_copy(p, core, 4).start())

    def act_ready(p):
        arrive(acts[p].at[0], r_s3.at[p])

    def act_done(p):
        s0_done(p)

        def go(core):
            for i in range(1, 4):
                s1_copy(p, i, at_y(i) if core == 0 else at_z(i)).wait_send()
            for w in range(4):
                s2_copy(p, core, w).wait_send()
            for w in range(5):
                s3_copy(p, core, w).wait_send()

        by_core(go)

    def a2a(q):
        dst = grads.at[q, k, zh, y, x, zl]

        def send(j, _):
            t = lax.rem(me // 2 + j, 16)
            begin = pl.multiple_of(t * ROWS + q * CH, CH)
            ty = t // 4
            tz = lax.rem(t, 4)

            @pl.when((j > 0) | (k == 1))
            def _():
                remote(
                    gate_in.at[:, pl.ds(begin, CH)], dst, s_a2a.at[q], r_a2a.at[q], device_of(x, ty, tz, 0)
                ).start()

            @pl.when((j > 0) | (k == 0))
            def _():
                remote(
                    up_in.at[:, pl.ds(begin, CH)], dst, s_a2a.at[q], r_a2a.at[q], device_of(x, ty, tz, 1)
                ).start()

            return 0

        begin = pl.multiple_of((me // 2) * ROWS + q * CH, CH)

        @pl.when(k == 0)
        def _():
            pltpu.make_async_copy(gate_in.at[:, pl.ds(begin, CH)], dst, r_a2a.at[q]).start()

        @pl.when(k == 1)
        def _():
            pltpu.make_async_copy(up_in.at[:, pl.ds(begin, CH)], dst, r_a2a.at[q]).start()

        lax.fori_loop(0, 16, send, 0)

    def ring_copy(q, which):
        at = [0, 0, 3, 1][which]
        xx = lax.rem(x + at, 4)
        ref = grads.at[q, :, :, :, xx] if which < 2 else grads.at[q, which - 2, :, :, xx]
        return remote(ref, ref, s_ring.at[q, which], r_ring.at[q, which], at_x(1 if which % 2 == 0 else 3))

    def ring(q):
        arrive(grads.at[q, :, :, :, 0], r_a2a.at[q])
        ring_copy(q, 0).start()
        ring_copy(q, 1).start()

    def ring_on(q):
        arrive(grads.at[q, :, :, :, 0], r_ring.at[q, 0])
        ring_copy(q, 2).start()
        arrive(grads.at[q, :, :, :, 0], r_ring.at[q, 1])
        ring_copy(q, 3).start()

    def grad_ready(q):
        arrive(grads.at[q, 0, :, :, 0], r_ring.at[q, 2])
        arrive(grads.at[q, 0, :, :, 0], r_ring.at[q, 3])

    def grad_done(q, _):
        sent = gate_in.at[:, pl.ds(0, 31 * CH)]
        pltpu.make_async_copy(sent, sent, s_a2a.at[q]).wait()
        for w in range(4):
            ring_copy(q, w).wait_send()
        return 0

    pair_of = lsr(lax.broadcasted_iota(jnp.int32, (256, 256), 1) & 15, 1)

    def work(q, p_lo, p_hi, between=lambda: None):
        def eight_docs(d, _):
            for c in range(2):
                for yy in range(4):
                    gt = grads[q, d, c, yy].reshape(SEQ, CH).T
                    for p in range(p_lo, p_hi):
                        a = acts[p][d, c, yy].reshape(SEQ, PIECE[p])
                        g = jnp.dot(gt, a, preferred_element_type=jnp.float32)
                        gs[d * 8 + c * 4 + yy, :, BEGIN[p]:BEGIN[p] + PIECE[p]] = g.astype(BF16)
            return 0

        lax.fori_loop(0, 2, eight_docs, 0)
        between()
        lo, hi = BEGIN[p_lo], BEGIN[p_hi - 1] + PIECE[p_hi - 1]

        def rows_32(t, _):
            for v in range(2):
                begin = pl.multiple_of(t * 32 + v * 16, 16)
                g = jnp.concatenate([gs[n, pl.ds(begin, 16), lo:hi] for n in range(16)], 0)
                picked = None
                for pair in range(8):
                    w = words[q * (CH // 2) + t * 16 + v * 8 + pair, :, lo:hi]
                    s = jnp.concatenate(
                        [
                            jnp.where(
                                (w & jnp.int16((1 << b) if b < 15 else -32768)) != 0, BF16(-1.0), BF16(1.0)
                            )
                            for b in range(16)
                        ],
                        0,
                    )
                    r = lax.dot_general(s, g, (((1,), (1,)), ((), ())), preferred_element_type=jnp.float32)
                    picked = r if picked is None else jnp.where(pair_of == pair, r, picked)
                acc[...] += picked
            return 0

        lax.fori_loop(0, CH // 32, rows_32, 0)

    acc[...] = jnp.zeros_like(acc)
    s0(0)
    a2a(0)
    s0(1)
    s0(2)
    hash_chunk(2)
    s1(0)
    hash_chunk(3)
    s2(0)
    ring(0)
    a2a(1)
    s1(1)
    hash_chunk(4)
    s2_on(0)
    s2(1)
    ring_on(0)
    hash_chunk(5)
    s3(0)
    ring(1)
    s1(2)
    a2a(2)
    hash_chunk(6)
    act_ready(0)
    grad_ready(0)
    work(0, 0, 1, lambda: s2_on(1))
    s2(2)
    s3(1)
    ring_on(1)
    act_ready(1)
    work(0, 1, 2, lambda: ring(2))
    a2a(3)

    def low(q, _):
        grad_ready(q)

        def between():
            @pl.when(q == 1)
            def _():
                s2_on(2)
                ring_on(2)

            @pl.when(q == 2)
            def _():
                ring(3)
                a2a(4)

        work(q, 0, 2, between)

        @pl.when(q == 1)
        def _():
            s3(2)

        return 0

    lax.fori_loop(1, 3, low, 0)
    act_ready(2)

    def high(q, _):
        def between():
            @pl.when(q == 1)
            def _():
                ring_on(3)
                ring(4)

        work(q, 2, 3, between)

        @pl.when(q < 2)
        def _():
            a2a(q + 5)

        return 0

    lax.fori_loop(0, 3, high, 0)

    def chunk(q, _):
        grad_ready(q)

        @pl.when(q + 1 < NQ)
        def _():
            ring_on(q + 1)

        @pl.when(q + 2 < NQ)
        def _():
            ring(q + 2)

        work(q, 0, 3)
        return 0

    lax.fori_loop(3, NQ, chunk, 0)

    ri = lax.broadcasted_iota(jnp.int32, (256, 256), 0)
    ci = lax.broadcasted_iota(jnp.int32, (256, 256), 1)
    kept = jnp.where((lsr(ri, 2) & 1) == (ci & 1), acc[...], 0.0)
    cf = lsr(lax.broadcasted_iota(jnp.int32, (256, 16), 0), 4)
    df = lax.broadcasted_iota(jnp.int32, (256, 16), 1)
    fold = jnp.zeros((256, 16), jnp.float32)
    for n in range(16):
        doc = order_ref[(n % 4) * 4 + ((n // 4) % 2) * 2 + n // 8]
        fold = jnp.where((cf == n) & (df == doc), 1.0, fold)
    rk = lax.broadcasted_iota(jnp.int32, (256, 128), 0)
    ck = lax.broadcasted_iota(jnp.int32, (256, 128), 1)
    place = jnp.where((rk & 3) * 32 + (lsr(rk, 3) & 1) * 16 + lsr(rk, 4) == ck, 1.0, 0.0)
    by_doc = jnp.dot(kept, fold, precision=lax.Precision.HIGHEST, preferred_element_type=jnp.float32)
    mine = lax.dot_general(
        by_doc, place, (((0,), (0,)), ((), ())),
        precision=lax.Precision.HIGHEST, preferred_element_type=jnp.float32,
    )
    for d in range(16):
        part[d] = jnp.broadcast_to(mine[d:d + 1, :], (8, 128))

    def f1_copy(j):
        t = lax.rem(row + j, 16)
        return remote(part.at[t], fin1.at[row], s_f1, r_f1, (t, col))

    pltpu.make_async_copy(part.at[row], fin1.at[row], r_f1).start()
    lax.fori_loop(1, 16, lambda j, _: (f1_copy(j).start(), 0)[1], 0)
    for p in range(NP):
        act_done(p)
    lax.fori_loop(0, NQ, grad_done, 0)
    arrive(fin1, r_f1)
    for m in range(2):
        total = fin1[m]
        for r in range(1, 8):
            total = total + fin1[r * 2 + m]
        mid[m] = total

    def f2_copy(j):
        return remote(mid, fin2.at[col], s_f2.at[j - 1], r_f2, (row, lax.rem(col + j, 8)))

    pltpu.make_async_copy(mid, fin2.at[col], r_f2).start()
    for j in range(1, 8):
        f2_copy(j).start()
    arrive(fin2, r_f2)
    total = fin2[0]
    for c in range(1, 8):
        total = total + fin2[c]
    out_ref[...] = total * (1.0 / math.sqrt(SEQ * D * FF))

    sent = part.at[pl.ds(0, 15)]
    pltpu.make_async_copy(sent, sent, s_f1).wait()
    for j in range(1, 8):
        f2_copy(j).wait_send()


def shards(activations, grad_gate, grad_up, doc_order, seeds):
    dma = pltpu.SemaphoreType.DMA
    total = pl.pallas_call(
        kernel,
        out_shape=jax.ShapeDtypeStruct((2, 8, K), jnp.float32),
        in_specs=[pl.BlockSpec(memory_space=pl.ANY)] * 3 + [pl.BlockSpec(memory_space=pltpu.SMEM)] * 2,
        out_specs=pl.BlockSpec(memory_space=pltpu.VMEM),
        scratch_shapes=[
            *[pltpu.VMEM((2, 2, 4, 4, 2, 32, width), BF16) for width in PIECE],
            pltpu.VMEM((NQ, 2, 2, 4, 4, 2, 32, CH), BF16),
            pltpu.VMEM((ROWS // 2, 16, COLS), jnp.int16),
            pltpu.VMEM((16, CH, COLS), BF16),
            pltpu.VMEM((256, 256), jnp.float32),
            pltpu.VMEM((16, 8, K), jnp.float32),
            pltpu.VMEM((16, 8, K), jnp.float32),
            pltpu.VMEM((2, 8, K), jnp.float32),
            pltpu.VMEM((8, 2, 8, K), jnp.float32),
            dma((NP,)), dma((NP,)), dma((NP, 4)), dma((NP,)), dma((NQ,)), dma((NQ, 4)), dma, dma,
            dma((NP, 3)), dma((NP, 3)), dma((NP, 4)), dma((NP, 5)), dma((NQ,)), dma((NQ, 4)), dma, dma((7,)),
        ],
        compiler_params=pltpu.CompilerParams(
            collective_id=0, has_side_effects=True, vmem_limit_bytes=56 * 2**20
        ),
        name="sketch",
    )(activations, grad_gate, grad_up, doc_order, seeds)
    col = lax.axis_index("col")
    return lax.dynamic_slice(total, (jnp.int32(0), jnp.int32(0), col * 16), (2, 1, 16))


def solution(mesh):
    in_specs = (P(("row", "col"), None), P(("row", "col"), None), P(("row", "col"), None), P(), P())
    out_specs = P(None, "row", "col")
    return jax.shard_map(shards, mesh=mesh, in_specs=in_specs, out_specs=out_specs, check_vma=False)
```

```python
import functools
import math

import jax
import jax.numpy as jnp
from jax import lax
from jax.experimental import pallas as pl
from jax.experimental.pallas import tpu as pltpu
from jax.sharding import PartitionSpec as P

D = 4096
FF = 14336
K = 128
SEQ = 256
MESH = pl.DeviceIdType.MESH
BF16 = jnp.bfloat16
ROWS = 896
COLS = 1024
CH = 128
NQ = ROWS // CH
PIECE = (256, 256, 512)
BEGIN = (0, 256, 512)
NP = 3


def lsr(value, count):
    return lax.shift_right_logical(value, jnp.full_like(value, count))


def hash_mix(v):
    v = v ^ lsr(v, 16)
    v = v * -2048144789
    v = v ^ lsr(v, 13)
    v = v * -1028477387
    return v ^ lsr(v, 16)


def device_of(x, y, z, k):
    return (y * 4 + (z // 2) * 2 + k, x * 2 + lax.rem(z, 2))


def kernel(
    act_in, gate_in, up_in, order_ref, seed_ref, out_ref,
    acts0, acts1, acts2, grads, words, gs, acc, part, fin1, mid, fin2,
    r_s0, r_s1, r_s2, r_s3, r_a2a, r_ring, r_f1, r_f2,
    s_s0, s_s1, s_s2, s_s3, s_a2a, s_ring, s_f1, s_f2,
):
    acts = (acts0, acts1, acts2)
    row = lax.axis_index("row")
    col = lax.axis_index("col")
    y = row // 4
    zh = lax.rem(row // 2, 2)
    k = lax.rem(row, 2)
    x = col // 2
    zl = lax.rem(col, 2)
    z = zh * 2 + zl
    me = (y * 4 + z) * 2 + k

    def at_x(dx):
        return device_of(lax.rem(x + dx, 4), y, z, k)

    def at_y(dy):
        return device_of(x, lax.rem(y + dy, 4), z, k)

    def at_z(dz):
        return device_of(x, y, lax.rem(z + dz, 4), k)

    sibling = device_of(x, y, z, 1 - k)

    barrier = pltpu.get_barrier_semaphore()

    def greet(j, _):
        t = lax.rem(me + j, 32)
        pl.semaphore_signal(
            barrier, inc=1, device_id=device_of(x, t // 8, lax.rem(t // 2, 4), lax.rem(t, 2)), device_id_type=MESH
        )
        return 0

    lax.fori_loop(1, 32, greet, 0)
    for dx in range(1, 4):
        for dz in range(2):
            pl.semaphore_signal(
                barrier, inc=1,
                device_id=(row, lax.rem(x + dx, 4) * 2 + lax.rem(zl + dz, 2)), device_id_type=MESH,
            )
    seed = jnp.where(k == 0, seed_ref[0], seed_ref[1])
    row_base = (y * 4 + z) * ROWS
    col_base = x * COLS

    def hash_chunk(q):
        it = lax.broadcasted_iota(jnp.int32, (8, COLS), 0)
        jt = lax.broadcasted_iota(jnp.int32, (8, COLS), 1)
        base = ((row_base + lsr(it, 2)) * D + col_base + jt) * 4 + (it & 3)

        def two_rows(t, _):
            for u in range(2):
                tt = q * (CH // 2) + t * 2 + u
                h = hash_mix(hash_mix(base + tt * (2 * D * 4)) + seed)
                words[tt] = jnp.concatenate([h, lsr(h, 16)], 0).astype(jnp.int16)
            return 0

        lax.fori_loop(0, CH // 4, two_rows, 0)

    hash_chunk(0)
    hash_chunk(1)
    pl.semaphore_wait(barrier, 37)

    def remote(src, dst, send, recv, target):
        return pltpu.make_async_remote_copy(
            src_ref=src, dst_ref=dst, send_sem=send, recv_sem=recv, device_id=target, device_id_type=MESH
        )

    def arrive(ref, sem):
        pltpu.make_async_copy(ref, ref, sem).wait()

    def act_slice(c):
        return lambda p: act_in.at[:, pl.ds(pl.multiple_of(c * COLS + BEGIN[p], 256), PIECE[p])]

    def s0(p):
        own = acts[p].at[k, zh, y, x, zl]
        pltpu.make_async_copy(act_slice(x)(p), own, r_s0.at[p]).start()
        for dx in range(1, 4):
            c = lax.rem(x + dx, 4)
            remote(act_slice(c)(p), own, s_s0.at[p, dx - 1], r_s0.at[p], at_x(dx)).start()

    def s0_done(p):
        for dx in range(1, 4):
            own = acts[p].at[k, zh, y, x, zl]
            remote(act_slice(lax.rem(x + dx, 4))(p), own, s_s0.at[p, dx - 1], r_s0.at[p], at_x(dx)).wait_send()

    def s1_copy(p, i, target):
        block = acts[p].at[k, zh, y, :, zl]
        return remote(block, block, s_s1.at[p, i - 1], r_s1.at[p], target)

    def s1(p):
        arrive(acts[p].at[0, 0, 0, :, 0], r_s0.at[p])

        @pl.when(k == 0)
        def _():
            for i in range(1, 4):
                s1_copy(p, i, at_y(i)).start()

        @pl.when(k == 1)
        def _():
            for i in range(1, 4):
                s1_copy(p, i, at_z(i)).start()

    def line(p, core, step, half=None):
        if core == 0:
            zz = lax.rem(z + step, 4)
            ys = pl.ds(0, 4) if half is None else pl.ds(half * 2, 2)
            return acts[p].at[0, zz // 2, ys, :, lax.rem(zz, 2)]
        yy = lax.rem(y + step, 4)
        if half is None:
            return acts[p].at[1, :, yy]
        return acts[p].at[1, half, yy]

    def nxt(core, step):
        return at_z(step) if core == 0 else at_y(step)

    def s2_copy(p, core, which):
        ref = [line(p, core, 0), line(p, core, 0), line(p, core, 3, 0), line(p, core, 1, 1)][which]
        return remote(ref, ref, s_s2.at[p, which], r_s2.at[p, which], nxt(core, 1 if which % 2 == 0 else 3))

    def s3_copy(p, core, which):
        ref = [
            line(p, core, 0), line(p, core, 3), line(p, core, 1), line(p, core, 2, 0), line(p, core, 2, 1)
        ][which]
        return remote(ref, ref, s_s3.at[p, which], r_s3.at[p], sibling)

    def by_core(f):
        @pl.when(k == 0)
        def _():
            f(0)

        @pl.when(k == 1)
        def _():
            f(1)

    full = lambda p: acts[p].at[0, 0, :, :, 0]
    half = lambda p: acts[p].at[0, 0, pl.ds(0, 2), :, 0]

    def s2(p):
        arrive(acts[p].at[0, 0, pl.ds(0, 3), :, 0], r_s1.at[p])

        def go(core):
            s2_copy(p, core, 0).start()
            s2_copy(p, core, 1).start()
            s3_copy(p, core, 0).start()

        by_core(go)

    def s2_on(p):
        arrive(full(p), r_s2.at[p, 0])

        def go_left(core):
            s2_copy(p, core, 2).start()
            s3_copy(p, core, 1).start()

        by_core(go_left)
        arrive(full(p), r_s2.at[p, 1])

        def go_right(core):
            s2_copy(p, core, 3).start()
            s3_copy(p, core, 2).start()

        by_core(go_right)

    def s3(p):
        arrive(half(p), r_s2.at[p, 2])
        by_core(lambda core: s3_copy(p, core, 3).start())
        arrive(half(p), r_s2.at[p, 3])
        by_core(lambda core: s3_copy(p, core, 4).start())

    def act_ready(p):
        arrive(acts[p].at[0], r_s3.at[p])

    def act_done(p):
        s0_done(p)

        def go(core):
            for i in range(1, 4):
                s1_copy(p, i, at_y(i) if core == 0 else at_z(i)).wait_send()
            for w in range(4):
                s2_copy(p, core, w).wait_send()
            for w in range(5):
                s3_copy(p, core, w).wait_send()

        by_core(go)

    def a2a(q):
        dst = grads.at[q, k, zh, y, x, zl]

        def send(j, _):
            t = lax.rem(me // 2 + j, 16)
            begin = pl.multiple_of(t * ROWS + q * CH, CH)
            ty = t // 4
            tz = lax.rem(t, 4)

            @pl.when((j > 0) | (k == 1))
            def _():
                remote(
                    gate_in.at[:, pl.ds(begin, CH)], dst, s_a2a.at[q], r_a2a.at[q], device_of(x, ty, tz, 0)
                ).start()

            @pl.when((j > 0) | (k == 0))
            def _():
                remote(
                    up_in.at[:, pl.ds(begin, CH)], dst, s_a2a.at[q], r_a2a.at[q], device_of(x, ty, tz, 1)
                ).start()

            return 0

        begin = pl.multiple_of((me // 2) * ROWS + q * CH, CH)

        @pl.when(k == 0)
        def _():
            pltpu.make_async_copy(gate_in.at[:, pl.ds(begin, CH)], dst, r_a2a.at[q]).start()

        @pl.when(k == 1)
        def _():
            pltpu.make_async_copy(up_in.at[:, pl.ds(begin, CH)], dst, r_a2a.at[q]).start()

        lax.fori_loop(0, 16, send, 0)

    def ring_copy(q, which):
        at = [0, 0, 3, 1][which]
        xx = lax.rem(x + at, 4)
        ref = grads.at[q, :, :, :, xx] if which < 2 else grads.at[q, which - 2, :, :, xx]
        return remote(ref, ref, s_ring.at[q, which], r_ring.at[q, which], at_x(1 if which % 2 == 0 else 3))

    def ring(q):
        arrive(grads.at[q, :, :, :, 0], r_a2a.at[q])
        ring_copy(q, 0).start()
        ring_copy(q, 1).start()

    def ring_on(q):
        arrive(grads.at[q, :, :, :, 0], r_ring.at[q, 0])
        ring_copy(q, 2).start()
        arrive(grads.at[q, :, :, :, 0], r_ring.at[q, 1])
        ring_copy(q, 3).start()

    def grad_ready(q):
        arrive(grads.at[q, 0, :, :, 0], r_ring.at[q, 2])
        arrive(grads.at[q, 0, :, :, 0], r_ring.at[q, 3])

    def grad_done(q, _):
        sent = gate_in.at[:, pl.ds(0, 31 * CH)]
        pltpu.make_async_copy(sent, sent, s_a2a.at[q]).wait()
        for w in range(4):
            ring_copy(q, w).wait_send()
        return 0

    pair_of = lsr(lax.broadcasted_iota(jnp.int32, (256, 256), 1) & 15, 1)

    def work(q, p_lo, p_hi, between=lambda: None):
        def eight_docs(d, _):
            for c in range(2):
                for yy in range(4):
                    gt = grads[q, d, c, yy].reshape(SEQ, CH).T
                    for p in range(p_lo, p_hi):
                        a = acts[p][d, c, yy].reshape(SEQ, PIECE[p])
                        g = jnp.dot(gt, a, preferred_element_type=jnp.float32)
                        gs[d * 8 + c * 4 + yy, :, BEGIN[p]:BEGIN[p] + PIECE[p]] = g.astype(BF16)
            return 0

        eight_docs(0, 0)
        eight_docs(1, 0)
        between()
        lo, hi = BEGIN[p_lo], BEGIN[p_hi - 1] + PIECE[p_hi - 1]

        def rows_64(t, _):
            for v in range(4):
                begin = pl.multiple_of(t * 64 + v * 16, 16)
                g = jnp.concatenate([gs[n, pl.ds(begin, 16), lo:hi] for n in range(16)], 0)
                picked = None
                for pair in range(8):
                    w = words[q * (CH // 2) + t * 32 + v * 8 + pair, :, lo:hi]
                    s = jnp.concatenate(
                        [
                            jnp.where(
                                (w & jnp.int16((1 << b) if b < 15 else -32768)) != 0, BF16(-1.0), BF16(1.0)
                            )
                            for b in range(16)
                        ],
                        0,
                    )
                    r = lax.dot_general(s, g, (((1,), (1,)), ((), ())), preferred_element_type=jnp.float32)
                    picked = r if picked is None else jnp.where(pair_of == pair, r, picked)
                acc[...] += picked
            return 0

        lax.fori_loop(0, CH // 64, rows_64, 0)

    acc[...] = jnp.zeros_like(acc)
    s0(0)
    a2a(0)
    s0(1)
    s0(2)
    hash_chunk(2)
    s1(0)
    hash_chunk(3)
    s2(0)
    ring(0)
    a2a(1)
    s1(1)
    hash_chunk(4)
    s2_on(0)
    s2(1)
    ring_on(0)
    hash_chunk(5)
    s3(0)
    ring(1)
    s1(2)
    a2a(2)
    act_ready(0)
    grad_ready(0)
    work(0, 0, 1, lambda: s2_on(1))
    s2(2)
    s3(1)
    ring_on(1)
    act_ready(1)
    work(0, 1, 2, lambda: ring(2))
    a2a(3)

    def low(q, _):
        grad_ready(q)

        def between():
            @pl.when(q == 1)
            def _():
                s2_on(2)
                hash_chunk(6)
                ring_on(2)

            @pl.when(q == 2)
            def _():
                ring(3)
                a2a(4)

        work(q, 0, 2, between)

        @pl.when(q == 1)
        def _():
            s3(2)

        return 0

    lax.fori_loop(1, 3, low, 0)
    act_ready(2)

    def high(q, _):
        def between():
            @pl.when(q == 1)
            def _():
                ring_on(3)
                ring(4)

        work(q, 2, 3, between)

        @pl.when(q < 2)
        def _():
            a2a(q + 5)

        return 0

    lax.fori_loop(0, 3, high, 0)

    def chunk(q, _):
        grad_ready(q)

        @pl.when(q + 1 < NQ)
        def _():
            ring_on(q + 1)

        @pl.when(q + 2 < NQ)
        def _():
            ring(q + 2)

        work(q, 0, 3)
        return 0

    lax.fori_loop(3, NQ, chunk, 0)

    ri = lax.broadcasted_iota(jnp.int32, (256, 256), 0)
    ci = lax.broadcasted_iota(jnp.int32, (256, 256), 1)
    kept = jnp.where((lsr(ri, 2) & 1) == (ci & 1), acc[...], 0.0)
    cf = lsr(lax.broadcasted_iota(jnp.int32, (256, 16), 0), 4)
    df = lax.broadcasted_iota(jnp.int32, (256, 16), 1)
    fold = jnp.zeros((256, 16), jnp.float32)
    for n in range(16):
        doc = order_ref[(n % 4) * 4 + ((n // 4) % 2) * 2 + n // 8]
        fold = jnp.where((cf == n) & (df == doc), 1.0, fold)
    rk = lax.broadcasted_iota(jnp.int32, (256, 128), 0)
    ck = lax.broadcasted_iota(jnp.int32, (256, 128), 1)
    place = jnp.where((rk & 3) * 32 + (lsr(rk, 3) & 1) * 16 + lsr(rk, 4) == ck, 1.0, 0.0)
    by_doc = jnp.dot(kept, fold, precision=lax.Precision.HIGHEST, preferred_element_type=jnp.float32)
    mine = lax.dot_general(
        by_doc, place, (((0,), (0,)), ((), ())),
        precision=lax.Precision.HIGHEST, preferred_element_type=jnp.float32,
    )
    for d in range(16):
        part[d] = jnp.broadcast_to(mine[d:d + 1, :], (8, 128))

    def f1_copy(j):
        t = lax.rem(row + j, 16)
        return remote(part.at[t], fin1.at[row], s_f1, r_f1, (t, col))

    pltpu.make_async_copy(part.at[row], fin1.at[row], r_f1).start()
    lax.fori_loop(1, 16, lambda j, _: (f1_copy(j).start(), 0)[1], 0)
    for p in range(NP):
        act_done(p)
    lax.fori_loop(0, NQ, grad_done, 0)
    arrive(fin1, r_f1)
    for m in range(2):
        total = fin1[m]
        for r in range(1, 8):
            total = total + fin1[r * 2 + m]
        mid[m] = total

    def f2_copy(j):
        return remote(mid, fin2.at[col], s_f2.at[j - 1], r_f2, (row, lax.rem(col + j, 8)))

    pltpu.make_async_copy(mid, fin2.at[col], r_f2).start()
    for j in range(1, 8):
        f2_copy(j).start()
    arrive(fin2, r_f2)
    total = fin2[0]
    for c in range(1, 8):
        total = total + fin2[c]
    out_ref[...] = total * (1.0 / math.sqrt(SEQ * D * FF))

    sent = part.at[pl.ds(0, 15)]
    pltpu.make_async_copy(sent, sent, s_f1).wait()
    for j in range(1, 8):
        f2_copy(j).wait_send()


def shards(activations, grad_gate, grad_up, doc_order, seeds):
    dma = pltpu.SemaphoreType.DMA
    total = pl.pallas_call(
        kernel,
        out_shape=jax.ShapeDtypeStruct((2, 8, K), jnp.float32),
        in_specs=[pl.BlockSpec(memory_space=pl.ANY)] * 3 + [pl.BlockSpec(memory_space=pltpu.SMEM)] * 2,
        out_specs=pl.BlockSpec(memory_space=pltpu.VMEM),
        scratch_shapes=[
            *[pltpu.VMEM((2, 2, 4, 4, 2, 32, width), BF16) for width in PIECE],
            pltpu.VMEM((NQ, 2, 2, 4, 4, 2, 32, CH), BF16),
            pltpu.VMEM((ROWS // 2, 16, COLS), jnp.int16),
            pltpu.VMEM((16, CH, COLS), BF16),
            pltpu.VMEM((256, 256), jnp.float32),
            pltpu.VMEM((16, 8, K), jnp.float32),
            pltpu.VMEM((16, 8, K), jnp.float32),
            pltpu.VMEM((2, 8, K), jnp.float32),
            pltpu.VMEM((8, 2, 8, K), jnp.float32),
            dma((NP,)), dma((NP,)), dma((NP, 4)), dma((NP,)), dma((NQ,)), dma((NQ, 4)), dma, dma,
            dma((NP, 3)), dma((NP, 3)), dma((NP, 4)), dma((NP, 5)), dma((NQ,)), dma((NQ, 4)), dma, dma((7,)),
        ],
        compiler_params=pltpu.CompilerParams(
            collective_id=0, has_side_effects=True, vmem_limit_bytes=56 * 2**20
        ),
        name="sketch",
    )(activations, grad_gate, grad_up, doc_order, seeds)
    col = lax.axis_index("col")
    return lax.dynamic_slice(total, (jnp.int32(0), jnp.int32(0), col * 16), (2, 1, 16))


def solution(mesh):
    in_specs = (P(("row", "col"), None), P(("row", "col"), None), P(("row", "col"), None), P(), P())
    out_specs = P(None, "row", "col")
    return jax.shard_map(shards, mesh=mesh, in_specs=in_specs, out_specs=out_specs, check_vma=False)
```

```python
import functools
import math

import jax
import jax.numpy as jnp
from jax import lax
from jax.experimental import pallas as pl
from jax.experimental.pallas import tpu as pltpu
from jax.sharding import PartitionSpec as P

D = 4096
FF = 14336
K = 128
SEQ = 256
MESH = pl.DeviceIdType.MESH
BF16 = jnp.bfloat16
ROWS = 896
COLS = 1024
CH = 128
NQ = ROWS // CH
PIECE = (256, 256, 512)
BEGIN = (0, 256, 512)
NP = 3


def lsr(value, count):
    return lax.shift_right_logical(value, jnp.full_like(value, count))


def hash_mix(v):
    v = v ^ lsr(v, 16)
    v = v * -2048144789
    v = v ^ lsr(v, 13)
    v = v * -1028477387
    return v ^ lsr(v, 16)


def device_of(x, y, z, k):
    return (y * 4 + (z // 2) * 2 + k, x * 2 + lax.rem(z, 2))


def kernel(
    act_in, gate_in, up_in, order_ref, seed_ref, out_ref,
    acts0, acts1, acts2, grads, words, gs, acc, part, fin1, mid, fin2,
    r_s0, r_s1, r_s2, r_s3, r_a2a, r_ring, r_f1, r_f2,
    s_s0, s_s1, s_s2, s_s3, s_a2a, s_ring, s_f1, s_f2,
):
    acts = (acts0, acts1, acts2)
    row = lax.axis_index("row")
    col = lax.axis_index("col")
    y = row // 4
    zh = lax.rem(row // 2, 2)
    k = lax.rem(row, 2)
    x = col // 2
    zl = lax.rem(col, 2)
    z = zh * 2 + zl
    me = (y * 4 + z) * 2 + k

    def at_x(dx):
        return device_of(lax.rem(x + dx, 4), y, z, k)

    def at_y(dy):
        return device_of(x, lax.rem(y + dy, 4), z, k)

    def at_z(dz):
        return device_of(x, y, lax.rem(z + dz, 4), k)

    sibling = device_of(x, y, z, 1 - k)

    barrier = pltpu.get_barrier_semaphore()

    def greet(j, _):
        t = lax.rem(me + j, 32)
        pl.semaphore_signal(
            barrier, inc=1, device_id=device_of(x, t // 8, lax.rem(t // 2, 4), lax.rem(t, 2)), device_id_type=MESH
        )
        return 0

    lax.fori_loop(1, 32, greet, 0)
    for dx in range(1, 4):
        for dz in range(2):
            pl.semaphore_signal(
                barrier, inc=1,
                device_id=(row, lax.rem(x + dx, 4) * 2 + lax.rem(zl + dz, 2)), device_id_type=MESH,
            )
    seed = jnp.where(k == 0, seed_ref[0], seed_ref[1])
    row_base = (y * 4 + z) * ROWS
    col_base = x * COLS

    def hash_chunk(q):
        it = lax.broadcasted_iota(jnp.int32, (8, COLS), 0)
        jt = lax.broadcasted_iota(jnp.int32, (8, COLS), 1)
        base = ((row_base + lsr(it, 2)) * D + col_base + jt) * 4 + (it & 3)

        def two_rows(t, _):
            for u in range(2):
                tt = q * (CH // 2) + t * 2 + u
                h = hash_mix(hash_mix(base + tt * (2 * D * 4)) + seed)
                words[tt] = jnp.concatenate([h, lsr(h, 16)], 0).astype(jnp.int16)
            return 0

        lax.fori_loop(0, CH // 4, two_rows, 0)

    hash_chunk(0)
    hash_chunk(1)
    pl.semaphore_wait(barrier, 37)

    def remote(src, dst, send, recv, target):
        return pltpu.make_async_remote_copy(
            src_ref=src, dst_ref=dst, send_sem=send, recv_sem=recv, device_id=target, device_id_type=MESH
        )

    def arrive(ref, sem):
        pltpu.make_async_copy(ref, ref, sem).wait()

    def act_slice(c):
        return lambda p: act_in.at[:, pl.ds(pl.multiple_of(c * COLS + BEGIN[p], 256), PIECE[p])]

    def s0(p):
        own = acts[p].at[k, zh, zl, y, x]
        pltpu.make_async_copy(act_slice(x)(p), own, r_s0.at[p]).start()
        for dx in range(1, 4):
            c = lax.rem(x + dx, 4)
            remote(act_slice(c)(p), own, s_s0.at[p, dx - 1], r_s0.at[p], at_x(dx)).start()

    def s0_done(p):
        for dx in range(1, 4):
            own = acts[p].at[k, zh, zl, y, x]
            remote(act_slice(lax.rem(x + dx, 4))(p), own, s_s0.at[p, dx - 1], r_s0.at[p], at_x(dx)).wait_send()

    def s1_copy(p, i, target):
        block = acts[p].at[k, zh, zl, y]
        return remote(block, block, s_s1.at[p, i - 1], r_s1.at[p], target)

    def s1(p):
        arrive(acts[p].at[0, 0, 0, 0], r_s0.at[p])

        @pl.when(k == 0)
        def _():
            for i in range(1, 4):
                s1_copy(p, i, at_y(i)).start()

        @pl.when(k == 1)
        def _():
            for i in range(1, 4):
                s1_copy(p, i, at_z(i)).start()

    def line(p, core, step, half=None):
        if core == 0:
            zz = lax.rem(z + step, 4)
            ys = pl.ds(0, 4) if half is None else pl.ds(half * 2, 2)
            return acts[p].at[0, zz // 2, lax.rem(zz, 2), ys]
        yy = lax.rem(y + step, 4)
        if half is None:
            return acts[p].at[1, :, :, yy]
        return acts[p].at[1, half, :, yy]

    def nxt(core, step):
        return at_z(step) if core == 0 else at_y(step)

    def s2_copy(p, core, which):
        ref = [line(p, core, 0), line(p, core, 0), line(p, core, 3, 0), line(p, core, 1, 1)][which]
        return remote(ref, ref, s_s2.at[p, which], r_s2.at[p, which], nxt(core, 1 if which % 2 == 0 else 3))

    def s3_copy(p, core, which):
        ref = [
            line(p, core, 0), line(p, core, 3), line(p, core, 1), line(p, core, 2, 0), line(p, core, 2, 1)
        ][which]
        return remote(ref, ref, s_s3.at[p, which], r_s3.at[p], sibling)

    def by_core(f):
        @pl.when(k == 0)
        def _():
            f(0)

        @pl.when(k == 1)
        def _():
            f(1)

    full = lambda p: acts[p].at[0, 0, 0]
    half = lambda p: acts[p].at[0, 0, 0, pl.ds(0, 2)]

    def s2(p):
        arrive(acts[p].at[0, 0, 0, pl.ds(0, 3)], r_s1.at[p])

        def go(core):
            s2_copy(p, core, 0).start()
            s2_copy(p, core, 1).start()
            s3_copy(p, core, 0).start()

        by_core(go)

    def s2_on(p):
        arrive(full(p), r_s2.at[p, 0])

        def go_left(core):
            s2_copy(p, core, 2).start()
            s3_copy(p, core, 1).start()

        by_core(go_left)
        arrive(full(p), r_s2.at[p, 1])

        def go_right(core):
            s2_copy(p, core, 3).start()
            s3_copy(p, core, 2).start()

        by_core(go_right)

    def s3(p):
        arrive(half(p), r_s2.at[p, 2])
        by_core(lambda core: s3_copy(p, core, 3).start())
        arrive(half(p), r_s2.at[p, 3])
        by_core(lambda core: s3_copy(p, core, 4).start())

    def act_ready(p):
        arrive(acts[p].at[0], r_s3.at[p])

    def act_done(p):
        s0_done(p)

        def go(core):
            for i in range(1, 4):
                s1_copy(p, i, at_y(i) if core == 0 else at_z(i)).wait_send()
            for w in range(4):
                s2_copy(p, core, w).wait_send()
            for w in range(5):
                s3_copy(p, core, w).wait_send()

        by_core(go)

    def a2a(q):
        dst = grads.at[q, k, zh, y, x, zl]

        def send(j, _):
            t = lax.rem(me // 2 + j, 16)
            begin = pl.multiple_of(t * ROWS + q * CH, CH)
            ty = t // 4
            tz = lax.rem(t, 4)

            @pl.when((j > 0) | (k == 1))
            def _():
                remote(
                    gate_in.at[:, pl.ds(begin, CH)], dst, s_a2a.at[q], r_a2a.at[q], device_of(x, ty, tz, 0)
                ).start()

            @pl.when((j > 0) | (k == 0))
            def _():
                remote(
                    up_in.at[:, pl.ds(begin, CH)], dst, s_a2a.at[q], r_a2a.at[q], device_of(x, ty, tz, 1)
                ).start()

            return 0

        begin = pl.multiple_of((me // 2) * ROWS + q * CH, CH)

        @pl.when(k == 0)
        def _():
            pltpu.make_async_copy(gate_in.at[:, pl.ds(begin, CH)], dst, r_a2a.at[q]).start()

        @pl.when(k == 1)
        def _():
            pltpu.make_async_copy(up_in.at[:, pl.ds(begin, CH)], dst, r_a2a.at[q]).start()

        lax.fori_loop(0, 16, send, 0)

    def ring_copy(q, which):
        at = [0, 0, 3, 1][which]
        xx = lax.rem(x + at, 4)
        ref = grads.at[q, :, :, :, xx] if which < 2 else grads.at[q, which - 2, :, :, xx]
        return remote(ref, ref, s_ring.at[q, which], r_ring.at[q, which], at_x(1 if which % 2 == 0 else 3))

    def ring(q):
        arrive(grads.at[q, :, :, :, 0], r_a2a.at[q])
        ring_copy(q, 0).start()
        ring_copy(q, 1).start()

    def ring_on(q):
        arrive(grads.at[q, :, :, :, 0], r_ring.at[q, 0])
        ring_copy(q, 2).start()
        arrive(grads.at[q, :, :, :, 0], r_ring.at[q, 1])
        ring_copy(q, 3).start()

    def grad_ready(q):
        arrive(grads.at[q, 0, :, :, 0], r_ring.at[q, 2])
        arrive(grads.at[q, 0, :, :, 0], r_ring.at[q, 3])

    def grad_done(q, _):
        sent = gate_in.at[:, pl.ds(0, 31 * CH)]
        pltpu.make_async_copy(sent, sent, s_a2a.at[q]).wait()
        for w in range(4):
            ring_copy(q, w).wait_send()
        return 0

    pair_of = lsr(lax.broadcasted_iota(jnp.int32, (256, 256), 1) & 15, 1)

    def work(q, p_lo, p_hi, between=lambda: None):
        def eight_docs(d, _):
            for c in range(2):
                for yy in range(4):
                    gt = jnp.concatenate([grads[q, d, c, yy, i % 4, i // 4] for i in range(8)], 0).T
                    for p in range(p_lo, p_hi):
                        a = acts[p][d, c, :, yy].reshape(SEQ, PIECE[p])
                        g = jnp.dot(gt, a, preferred_element_type=jnp.float32)
                        gs[d * 8 + c * 4 + yy, :, BEGIN[p]:BEGIN[p] + PIECE[p]] = g.astype(BF16)
            return 0

        eight_docs(0, 0)
        eight_docs(1, 0)
        between()
        lo, hi = BEGIN[p_lo], BEGIN[p_hi - 1] + PIECE[p_hi - 1]
        step = 64 if hi - lo == COLS else CH

        def some_rows(t, _):
            for v in range(step // 16):
                begin = pl.multiple_of(t * step + v * 16, 16)
                g = jnp.concatenate([gs[n, pl.ds(begin, 16), lo:hi] for n in range(16)], 0)
                picked = None
                for pair in range(8):
                    w = words[q * (CH // 2) + t * (step // 2) + v * 8 + pair, :, lo:hi]
                    s = jnp.concatenate(
                        [
                            jnp.where(
                                (w & jnp.int16((1 << b) if b < 15 else -32768)) != 0, BF16(-1.0), BF16(1.0)
                            )
                            for b in range(16)
                        ],
                        0,
                    )
                    r = lax.dot_general(s, g, (((1,), (1,)), ((), ())), preferred_element_type=jnp.float32)
                    picked = r if picked is None else jnp.where(pair_of == pair, r, picked)
                acc[...] += picked
            return 0

        lax.fori_loop(0, CH // step, some_rows, 0)

    acc[...] = jnp.zeros_like(acc)
    s0(0)
    a2a(0)
    s0(1)
    s0(2)
    hash_chunk(2)
    s1(0)
    hash_chunk(3)
    s2(0)
    ring(0)
    a2a(1)
    s1(1)
    hash_chunk(4)
    s2_on(0)
    s2(1)
    ring_on(0)
    hash_chunk(5)
    s3(0)
    ring(1)
    s1(2)
    a2a(2)
    act_ready(0)
    grad_ready(0)
    work(0, 0, 1, lambda: s2_on(1))
    s2(2)
    s3(1)
    ring_on(1)
    act_ready(1)
    work(0, 1, 2, lambda: ring(2))
    a2a(3)

    def low(q, _):
        grad_ready(q)

        def between():
            @pl.when(q == 1)
            def _():
                s2_on(2)
                hash_chunk(6)
                ring_on(2)

            @pl.when(q == 2)
            def _():
                ring(3)
                a2a(4)

        work(q, 0, 2, between)

        @pl.when(q == 1)
        def _():
            s3(2)

        return 0

    lax.fori_loop(1, 3, low, 0)
    act_ready(2)

    def high(q, _):
        def between():
            @pl.when(q == 1)
            def _():
                ring_on(3)
                ring(4)

        work(q, 2, 3, between)

        @pl.when(q < 2)
        def _():
            a2a(q + 5)

        return 0

    lax.fori_loop(0, 3, high, 0)

    def chunk(q, _):
        grad_ready(q)

        @pl.when(q + 1 < NQ)
        def _():
            ring_on(q + 1)

        @pl.when(q + 2 < NQ)
        def _():
            ring(q + 2)

        work(q, 0, 3)
        return 0

    lax.fori_loop(3, NQ, chunk, 0)

    ri = lax.broadcasted_iota(jnp.int32, (256, 256), 0)
    ci = lax.broadcasted_iota(jnp.int32, (256, 256), 1)
    kept = jnp.where((lsr(ri, 2) & 1) == (ci & 1), acc[...], 0.0)
    cf = lsr(lax.broadcasted_iota(jnp.int32, (256, 16), 0), 4)
    df = lax.broadcasted_iota(jnp.int32, (256, 16), 1)
    fold = jnp.zeros((256, 16), jnp.float32)
    for n in range(16):
        doc = order_ref[(n % 4) * 4 + ((n // 4) % 2) * 2 + n // 8]
        fold = jnp.where((cf == n) & (df == doc), 1.0, fold)
    rk = lax.broadcasted_iota(jnp.int32, (256, 128), 0)
    ck = lax.broadcasted_iota(jnp.int32, (256, 128), 1)
    place = jnp.where((rk & 3) * 32 + (lsr(rk, 3) & 1) * 16 + lsr(rk, 4) == ck, 1.0, 0.0)
    by_doc = jnp.dot(kept, fold, precision=lax.Precision.HIGHEST, preferred_element_type=jnp.float32)
    mine = lax.dot_general(
        by_doc, place, (((0,), (0,)), ((), ())),
        precision=lax.Precision.HIGHEST, preferred_element_type=jnp.float32,
    )
    for d in range(16):
        part[d] = jnp.broadcast_to(mine[d:d + 1, :], (8, 128))

    def f1_copy(j):
        t = lax.rem(row + j, 16)
        return remote(part.at[t], fin1.at[row], s_f1, r_f1, (t, col))

    pltpu.make_async_copy(part.at[row], fin1.at[row], r_f1).start()
    lax.fori_loop(1, 16, lambda j, _: (f1_copy(j).start(), 0)[1], 0)
    for p in range(NP):
        act_done(p)
    lax.fori_loop(0, NQ, grad_done, 0)
    arrive(fin1, r_f1)
    for m in range(2):
        total = fin1[m]
        for r in range(1, 8):
            total = total + fin1[r * 2 + m]
        mid[m] = total

    def f2_copy(j):
        return remote(mid, fin2.at[col], s_f2.at[j - 1], r_f2, (row, lax.rem(col + j, 8)))

    pltpu.make_async_copy(mid, fin2.at[col], r_f2).start()
    for j in range(1, 8):
        f2_copy(j).start()
    arrive(fin2, r_f2)
    total = fin2[0]
    for c in range(1, 8):
        total = total + fin2[c]
    out_ref[...] = total * (1.0 / math.sqrt(SEQ * D * FF))

    sent = part.at[pl.ds(0, 15)]
    pltpu.make_async_copy(sent, sent, s_f1).wait()
    for j in range(1, 8):
        f2_copy(j).wait_send()


def shards(activations, grad_gate, grad_up, doc_order, seeds):
    dma = pltpu.SemaphoreType.DMA
    total = pl.pallas_call(
        kernel,
        out_shape=jax.ShapeDtypeStruct((2, 8, K), jnp.float32),
        in_specs=[pl.BlockSpec(memory_space=pl.ANY)] * 3 + [pl.BlockSpec(memory_space=pltpu.SMEM)] * 2,
        out_specs=pl.BlockSpec(memory_space=pltpu.VMEM),
        scratch_shapes=[
            *[pltpu.VMEM((2, 2, 2, 4, 4, 32, width), BF16) for width in PIECE],
            pltpu.VMEM((NQ, 2, 2, 4, 4, 2, 32, CH), BF16),
            pltpu.VMEM((ROWS // 2, 16, COLS), jnp.int16),
            pltpu.VMEM((16, CH, COLS), BF16),
            pltpu.VMEM((256, 256), jnp.float32),
            pltpu.VMEM((16, 8, K), jnp.float32),
            pltpu.VMEM((16, 8, K), jnp.float32),
            pltpu.VMEM((2, 8, K), jnp.float32),
            pltpu.VMEM((8, 2, 8, K), jnp.float32),
            dma((NP,)), dma((NP,)), dma((NP, 4)), dma((NP,)), dma((NQ,)), dma((NQ, 4)), dma, dma,
            dma((NP, 3)), dma((NP, 3)), dma((NP, 4)), dma((NP, 5)), dma((NQ,)), dma((NQ, 4)), dma, dma((7,)),
        ],
        compiler_params=pltpu.CompilerParams(
            collective_id=0, has_side_effects=True, vmem_limit_bytes=56 * 2**20
        ),
        name="sketch",
    )(activations, grad_gate, grad_up, doc_order, seeds)
    col = lax.axis_index("col")
    return lax.dynamic_slice(total, (jnp.int32(0), jnp.int32(0), col * 16), (2, 1, 16))


def solution(mesh):
    in_specs = (P(("row", "col"), None), P(("row", "col"), None), P(("row", "col"), None), P(), P())
    out_specs = P(None, "row", "col")
    return jax.shard_map(shards, mesh=mesh, in_specs=in_specs, out_specs=out_specs, check_vma=False)
```
